32 devices in a mesh: grp: 2 (over y), user: 4 (over z), blk: 2 (over x), sub: 2 (over core).
Axes of the slice: x: 2, y: 2, z: 4, core: 2. Of those that a mesh axis runs over, the one named last changes fastest.
Arguments:
- engagement: bfloat16 [24576, 512], P(('grp', 'blk', 'sub'), 'user'), parts along dimension 0, may hold values from -6 to 6
- pattern: int32 [192, 4], P(('grp', 'blk', 'sub')), parts along dimension 0, may hold values 0 or 1
- degree: int32 [24576], P(('grp', 'blk', 'sub')), parts along dimension 0, may hold values from 1 to 256
Outputs:
- cooccur: float32 [1024, 512], P(('grp', 'user'), ('blk', 'sub')), parts along dimension 0
The draws below stay inside these ranges and needn't reach their ends.
There are 2 independent parts, one for each index of `grp`. The reference program is written for one: setup_inputs(seed, part) draws one part's arguments, and reference() takes and returns one part's arrays. A program takes and returns all parts, laid end to end along the dimension named above; each array names one. Nothing has to cross between parts.
All inputs are finite; a program needn't handle non-finite values. No bound on the sum of `pattern` on one device may be relied on, other than what follows from the above.
Results may differ from the reference program's by a relative error of at most 0.00097.
Values may be sent and summed in bfloat16 or wider, within the bound.
A program may use at most 64 MiB of HBM per device.

```python
import jax
import jax.numpy as jnp
from jax import lax

BW = 128
UT = 128
U_DEV = 3072
BLOCKS = 4
ITEMS = 512
USERS = 12288
TILES = 96


def with_ends(array, key, low, top_value):
    longest = array.shape.index(max(array.shape))
    spots = []
    for shift in (0, 1):
        where = [jax.random.randint(jax.random.fold_in(key, axis), (), 0, length) for axis, length in enumerate(array.shape)]
        where[longest] = (where[longest] + shift) % array.shape[longest]
        spots.append(tuple(where))
    return array.at[spots[0]].set(low).at[spots[1]].set(top_value)


def levels(own_key, extent, cuts, smallest, top_value):
    loudness, own = 1.0, jax.random.fold_in(own_key, 6)
    for axis_at, parts in cuts:
        draws = jnp.exp(jax.random.uniform(jax.random.fold_in(own, axis_at), (parts,), jnp.float32, smallest / len(cuts), top_value / len(cuts)))
        loudness = loudness * jnp.repeat(draws, extent[axis_at] // parts).reshape([-1 if axis == axis_at else 1 for axis in range(len(extent))])
    return loudness


def normal_values(own_key, dims, scale, most, split=(), kind=jnp.bfloat16):
    level = levels(own_key, dims, split, -0.22, 0.18) if split else 1.0
    entries = jax.random.normal(own_key, dims, jnp.float32) * scale * level
    return jnp.minimum(jnp.maximum(entries, -most), most).astype(kind)


def setup_inputs(seed: int = 0, part: int = 0) -> dict:
    seeds = jax.random.split(jax.random.key(seed), 4)
    part_keys = jax.random.split(jax.random.fold_in(seeds[3], part), 4)
    return {
        "engagement": normal_values(part_keys[0], (USERS, ITEMS), 1.0, 6.0, ((0, 4), (1, 4))),
        "pattern": with_ends((jax.random.randint(part_keys[1], (TILES, BLOCKS), 0, 2) < 1).astype(jnp.int32), jax.random.fold_in(part_keys[1], 1), 0, 1),
        "degree": with_ends(jax.random.randint(part_keys[2], (USERS,), 1, 257), jax.random.fold_in(part_keys[2], 1), 1, 256).astype(jnp.int32),
    }


def reference(engagement, pattern, degree):
    tiles = USERS // UT
    mask = pattern.astype(jnp.bfloat16)
    masked = (engagement.reshape(tiles, UT, BLOCKS, BW) * mask[:, None, :, None]).reshape(USERS, ITEMS)
    weight = jnp.sqrt(lax.rsqrt(degree.astype(jnp.float32))) * float(USERS) ** (-0.25)
    left = (masked.astype(jnp.float32) * weight[:, None]).astype(jnp.bfloat16)
    steps_count = USERS // U_DEV
    left_blocks = left.reshape(steps_count, U_DEV, ITEMS)

    def accumulate(total, part_left):
        return (total + lax.dot_general(part_left, part_left, (((0,), (0,)), ((), ())), preferred_element_type=jnp.float32), None)
    full, unused = lax.scan(accumulate, jnp.zeros((ITEMS, ITEMS), jnp.float32), left_blocks)
    row_block = jnp.arange(ITEMS, dtype=jnp.int32) // BW
    keep = row_block[None, :] >= row_block[:, None]
    return jnp.where(keep, full, jnp.float32(0.0))
```

```python
import functools

import jax
import jax.numpy as jnp
from jax import lax
from jax.experimental import pallas as pl
from jax.experimental.pallas import tpu as pltpu
from jax.sharding import PartitionSpec as P

MESH = pl.DeviceIdType.MESH


def contract(first, second):
    return lax.dot_general(
        first, second, (((0,), (0,)), ((), ())), preferred_element_type=jnp.float32
    )


def pair_slot(n, i, j):
    return i * n - (i * (i + 1)) // 2 + (j - i - 1)


def kernel(
    n, nb, ns, chunks, eng_hbm, pattern_ref, degree_ref, out_ref,
    eng, left, acc, other, diag, landed,
    load_sem, in_send, in_recv, core_send, core_recv, out_send, out_recv, diag_send,
):
    g, z = lax.axis_index("grp"), lax.axis_index("user")
    x, c = lax.axis_index("blk"), lax.axis_index("sub")
    rows, width = eng.shape
    tiles = degree_ref.shape[0]
    tile = rows // tiles
    half = rows // 2
    step = half // chunks
    procs = (n // 2 - 1, n // 2)
    column = x * ns + c
    pairs = [(i, j) for i in range(n) for j in range(i + 1, n)]

    load = pltpu.make_async_copy(eng_hbm, eng, load_sem)
    load.start()

    barrier = pltpu.get_barrier_semaphore()
    everyone = n * nb * ns

    def greet(k, carry):
        zz, xx, cc = k // (nb * ns), (k // ns) % nb, k % ns

        @pl.when((zz != z) | (xx != x) | (cc != c))
        def _():
            pl.semaphore_signal(barrier, inc=1, device_id=(g, zz, xx, cc), device_id_type=MESH)

        return carry

    lax.fori_loop(0, everyone, greet, 0)

    lanes = lax.broadcasted_iota(jnp.int32, pattern_ref.shape, 1)
    mask = jnp.sum(jnp.where(lanes == z, pattern_ref[...], 0), axis=1, keepdims=True)
    weight = jnp.sqrt(lax.rsqrt(degree_ref[...].astype(jnp.float32)))
    weight = weight * float(rows * nb * ns) ** (-0.25) * mask.astype(jnp.float32)
    weight = weight.T

    load.wait()

    def prepare(p, k):
        start = p * half + k * step
        for t in range(start // tile, (start + step) // tile):
            at = pl.ds(t * tile, tile)
            scaled = eng[at, :].astype(jnp.float32) * weight[:, t : t + 1]
            left[z, at, :] = scaled.astype(jnp.bfloat16)

    def block_copy(source, p, k):
        at = pl.ds(p * half + k * step, step)
        return pltpu.make_async_remote_copy(
            src_ref=left.at[source, at, :],
            dst_ref=left.at[source, at, :],
            send_sem=in_send.at[p, k],
            recv_sem=in_recv.at[source, k],
            device_id=(g, procs[p] if isinstance(p, int) else procs[0] + p, x, c),
            device_id_type=MESH,
        )

    for k in range(chunks):
        for p in range(2):
            prepare(p, k)
        if k == 0:
            pl.semaphore_wait(barrier, everyone - 1)
        for p in range(2):

            @pl.when(z != procs[p])
            def _():
                block_copy(z, p, k).start()

    def diag_copy(slot):
        return pltpu.make_async_remote_copy(
            src_ref=diag,
            dst_ref=landed.at[slot],
            send_sem=diag_send,
            recv_sem=out_recv.at[slot],
            device_id=(g, z, z // ns, lax.rem(z, ns)),
            device_id_type=MESH,
        )

    diag[...] = contract(left[z], left[z])

    @pl.when(column != z)
    def _():
        diag_copy(c * nb + x).start()

    def core_copy(s):
        return pltpu.make_async_remote_copy(
            src_ref=acc.at[s],
            dst_ref=other.at[s],
            send_sem=core_send.at[s],
            recv_sem=core_recv.at[s],
            device_id=(g, z, x, 1 - c),
            device_id_type=MESH,
        )

    def out_copy(s, slot, i, j):
        return pltpu.make_async_remote_copy(
            src_ref=acc.at[s],
            dst_ref=landed.at[slot],
            send_sem=out_send.at[s],
            recv_sem=out_recv.at[slot],
            device_id=(g, i, j // ns, c),
            device_id_type=MESH,
        )

    is_proc = (z == procs[0]) | (z == procs[1])

    @pl.when(is_proc)
    def _():
        p = z - procs[0]
        acc[...] = jnp.zeros_like(acc)

        def multiply(k, carry):
            for i in range(n):

                @pl.when(z != i)
                def _():
                    block_copy(i, p, k).wait_recv()

            at = pl.ds(pl.multiple_of(p * half + k * step, 16), step)
            for s, (i, j) in enumerate(pairs):
                acc[s] += contract(left[i, at, :], left[j, at, :])
            return carry

        lax.fori_loop(0, chunks, multiply, 0)

        for s, (i, j) in enumerate(pairs):

            @pl.when(c != j % ns)
            def _():
                core_copy(s).start()

        for s, (i, j) in enumerate(pairs):

            @pl.when(c == j % ns)
            def _():
                core_copy(s).wait_recv()
                acc[s] += other[s]

                @pl.when((z != i) | (x != j // ns))
                def _():
                    out_copy(s, p * nb + x, i, j).start()

    @pl.when(column < z)
    def _():
        out_ref[...] = jnp.zeros_like(out_ref)

    @pl.when(column == z)
    def _():
        out_ref[...] = diag[...]
        for cc in range(ns):
            for xx in range(nb):

                @pl.when((xx != x) | (cc != c))
                def _():
                    slot = cc * nb + xx
                    diag_copy(slot).wait_recv()
                    out_ref[...] += landed[slot]

    @pl.when(column > z)
    def _():
        out_ref[...] = jnp.zeros_like(out_ref)

        @pl.when(is_proc)
        def _():
            out_ref[...] = acc[pair_slot(n, z, column)]

        for p in range(2):
            for xx in range(nb):

                @pl.when((z != procs[p]) | (xx != x))
                def _():
                    slot = p * nb + xx
                    out_copy(0, slot, z, column).wait_recv()
                    out_ref[...] += landed[slot]

    for k in range(chunks):
        for p in range(2):

            @pl.when(z != procs[p])
            def _():
                block_copy(z, p, k).wait_send()

    @pl.when(column != z)
    def _():
        diag_copy(0).wait_send()

    @pl.when(is_proc)
    def _():
        for s, (i, j) in enumerate(pairs):

            @pl.when(c != j % ns)
            def _():
                core_copy(s).wait_send()

            @pl.when((c == j % ns) & ((z != i) | (x != j // ns)))
            def _():
                out_copy(s, 0, i, j).wait_send()


def on_device(engagement, pattern, degree):
    n, nb, ns = lax.axis_size("user"), lax.axis_size("blk"), lax.axis_size("sub")
    rows, width = engagement.shape
    tiles = pattern.shape[0]
    assert n == nb * ns and ns == 2
    chunks = 6
    npairs = n * (n - 1) // 2
    block = (width, width)
    scratch = [
        pltpu.VMEM((rows, width), jnp.bfloat16),
        pltpu.VMEM((n, rows, width), jnp.bfloat16),
        pltpu.VMEM((npairs,) + block, jnp.float32),
        pltpu.VMEM((npairs,) + block, jnp.float32),
        pltpu.VMEM(block, jnp.float32),
        pltpu.VMEM((2 * nb,) + block, jnp.float32),
        pltpu.SemaphoreType.DMA,
        pltpu.SemaphoreType.DMA((2, chunks)),
        pltpu.SemaphoreType.DMA((n, chunks)),
        pltpu.SemaphoreType.DMA((npairs,)),
        pltpu.SemaphoreType.DMA((npairs,)),
        pltpu.SemaphoreType.DMA((npairs,)),
        pltpu.SemaphoreType.DMA((2 * nb,)),
        pltpu.SemaphoreType.DMA,
    ]
    vmem = pl.BlockSpec(memory_space=pltpu.VMEM)
    held = (n + 1) * rows * width * 2 + (2 * npairs + 2 * nb + 2) * width * width * 4
    return pl.pallas_call(
        functools.partial(kernel, n, nb, ns, chunks),
        out_shape=jax.ShapeDtypeStruct(block, jnp.float32),
        in_specs=[pl.BlockSpec(memory_space=pl.ANY), vmem, vmem],
        out_specs=vmem,
        scratch_shapes=scratch,
        compiler_params=pltpu.CompilerParams(
            collective_id=0, has_side_effects=True, vmem_limit_bytes=held + (12 << 20)
        ),
    )(engagement, pattern, degree.reshape(tiles, rows // tiles))


def solution(mesh):
    placed = (
        P(("grp", "blk", "sub"), "user"),
        P(("grp", "blk", "sub"), None),
        P(("grp", "blk", "sub")),
    )
    return jax.shard_map(
        on_device,
        mesh=mesh,
        in_specs=placed,
        out_specs=P(("grp", "user"), ("blk", "sub")),
        check_vma=False,
    )
```

```python
import functools

import jax
import jax.numpy as jnp
from jax import lax
from jax.experimental import pallas as pl
from jax.experimental.pallas import tpu as pltpu
from jax.sharding import PartitionSpec as P

MESH = pl.DeviceIdType.MESH


def contract(first, second):
    return lax.dot_general(
        first, second, (((0,), (0,)), ((), ())), preferred_element_type=jnp.float32
    )


def pair_slot(n, i, j):
    return i * n - (i * (i + 1)) // 2 + (j - i - 1)


def kernel(
    n, nb, ns, chunks, eng_hbm, pattern_ref, degree_ref, out_ref,
    eng, left, acc, other, diag, landed,
    load_sem, in_send, in_recv, core_send, core_recv, out_send, out_recv, diag_send,
):
    g, z = lax.axis_index("grp"), lax.axis_index("user")
    x, c = lax.axis_index("blk"), lax.axis_index("sub")
    rows, width = eng.shape
    tiles = degree_ref.shape[0]
    tile = rows // tiles
    half = rows // 2
    step = half // chunks
    procs = (n // 2 - 1, n // 2)
    column = x * ns + c
    is_proc = (z == procs[0]) | (z == procs[1])

    first = jnp.where((z < procs[0]) | (z == procs[1]), 0, 1)

    def load(p):
        at = pl.ds(pl.multiple_of(p * half, half), half)
        return pltpu.make_async_copy(eng_hbm.at[at, :], eng.at[at, :], load_sem.at[p])

    load(first).start()
    load(1 - first).start()

    barrier = pltpu.get_barrier_semaphore()

    def sends(source, target):
        (sz, sx, sc), (tz, tx, tc) = source, target
        source_proc = (sz == procs[0]) | (sz == procs[1])
        target_proc = (tz == procs[0]) | (tz == procs[1])
        block = target_proc & (sx == tx) & (sc == tc)
        core = source_proc & (sz == tz) & (sx == tx)
        pair = source_proc & (sc == tc) & (tz < tx * ns + tc)
        own = (sz == tz) & (tz == tx * ns + tc)
        same = (sz == tz) & (sx == tx) & (sc == tc)
        return (block | core | pair | own) & jnp.logical_not(same)

    def greet(k, count):
        device = (k // (nb * ns), (k // ns) % nb, k % ns)

        @pl.when(sends(device, (z, x, c)))
        def _():
            pl.semaphore_signal(barrier, inc=1, device_id=(g,) + device, device_id_type=MESH)

        return count + jnp.where(sends((z, x, c), device), 1, 0)

    targets = lax.fori_loop(0, n * nb * ns, greet, 0)

    mask = pattern_ref[pl.ds(z, 1), :].astype(jnp.float32)
    weight = jnp.sqrt(lax.rsqrt(degree_ref[...].astype(jnp.float32)))
    weight = (weight * float(rows * nb * ns) ** (-0.25)).T * mask

    def prepare(p, k):
        start = p * half + k * step
        for t in range(start // tile, (start + step) // tile):
            at = pl.ds(t * tile, tile)
            scaled = eng[at, :].astype(jnp.float32) * weight[:, t : t + 1]
            left[z, at, :] = scaled.astype(jnp.bfloat16)

    def block_copy(source, p, k):
        at = pl.ds(p * half + k * step, step)
        return pltpu.make_async_remote_copy(
            src_ref=left.at[source, at, :],
            dst_ref=left.at[source, at, :],
            send_sem=in_send.at[p, k],
            recv_sem=in_recv.at[source, k],
            device_id=(g, procs[p], x, c),
            device_id_type=MESH,
        )

    def send_half(p, k, greeted):
        prepare(p, k)
        if not greeted:
            pl.semaphore_wait(barrier, targets)

        @pl.when(z != procs[p])
        def _():
            block_copy(z, p, k).start()

    for p in range(2):

        @pl.when(first == p)
        def _():
            load(p).wait()
            for k in range(chunks):
                send_half(p, k, k > 0)
            load(1 - p).wait()
            for k in range(chunks):
                send_half(1 - p, k, True)

    def diag_copy(slot):
        return pltpu.make_async_remote_copy(
            src_ref=diag,
            dst_ref=landed.at[slot],
            send_sem=diag_send,
            recv_sem=out_recv.at[slot],
            device_id=(g, z, z // ns, lax.rem(z, ns)),
            device_id_type=MESH,
        )

    diag[...] = contract(left[z], left[z])

    @pl.when(column != z)
    def _():
        diag_copy(c * nb + x).start()

    def core_copy(s):
        return pltpu.make_async_remote_copy(
            src_ref=acc.at[s],
            dst_ref=other.at[s],
            send_sem=core_send.at[s],
            recv_sem=core_recv.at[s],
            device_id=(g, z, x, 1 - c),
            device_id_type=MESH,
        )

    def out_copy(s, slot, i, j):
        return pltpu.make_async_remote_copy(
            src_ref=acc.at[s],
            dst_ref=landed.at[slot],
            send_sem=out_send.at[s],
            recv_sem=out_recv.at[slot],
            device_id=(g, i, j // ns, c),
            device_id_type=MESH,
        )

    def pairs_of(p, blocks, pairs):
        for i, j in pairs:
            s = pair_slot(n, i, j)
            acc[s] = jnp.zeros_like(acc[s])

        def multiply(k, carry):
            for i in blocks:
                block_copy(i, p, k).wait_recv()
            at = pl.ds(pl.multiple_of(p * half + k * step, 16), step)
            for i, j in pairs:
                acc[pair_slot(n, i, j)] += contract(left[i, at, :], left[j, at, :])
            return carry

        lax.fori_loop(0, chunks, multiply, 0)

        for i, j in pairs:

            @pl.when(c != j % ns)
            def _():
                core_copy(pair_slot(n, i, j)).start()

        for i, j in pairs:
            s = pair_slot(n, i, j)

            @pl.when(c == j % ns)
            def _():
                core_copy(s).wait_recv()
                acc[s] += other[s]

                @pl.when((procs[p] != i) | (x != j // ns))
                def _():
                    out_copy(s, p * nb + x, i, j).start()

    pairs = [(i, j) for i in range(n) for j in range(i + 1, n)]
    for p in range(2):

        @pl.when(z == procs[p])
        def _():
            below, above = range(procs[0]), range(procs[1] + 1, n)
            near, far = (below, above) if p == 0 else (above, below)
            early = [pair for pair in pairs if not set(pair) & set(far)]
            late = sorted((pair for pair in pairs if set(pair) & set(far)), key=lambda pair: abs(pair[0] - procs[p]), reverse=True)
            pairs_of(p, [*near, procs[1 - p]], early)
            if late:
                pairs_of(p, far, late)

    @pl.when(column < z)
    def _():
        out_ref[...] = jnp.zeros_like(out_ref)

    @pl.when(column == z)
    def _():
        out_ref[...] = diag[...]
        for cc in range(ns):
            for xx in range(nb):

                @pl.when((xx != x) | (cc != c))
                def _():
                    slot = cc * nb + xx
                    diag_copy(slot).wait_recv()
                    out_ref[...] += landed[slot]

    @pl.when(column > z)
    def _():
        out_ref[...] = jnp.zeros_like(out_ref)

        @pl.when(is_proc)
        def _():
            out_ref[...] = acc[pair_slot(n, z, column)]

        for p in range(2):
            for xx in range(nb):

                @pl.when((z != procs[p]) | (xx != x))
                def _():
                    slot = p * nb + xx
                    out_copy(0, slot, z, column).wait_recv()
                    out_ref[...] += landed[slot]

    for k in range(chunks):
        for p in range(2):

            @pl.when(z != procs[p])
            def _():
                block_copy(z, p, k).wait_send()

    @pl.when(column != z)
    def _():
        diag_copy(0).wait_send()

    @pl.when(is_proc)
    def _():
        for s, (i, j) in enumerate(pairs):

            @pl.when(c != j % ns)
            def _():
                core_copy(s).wait_send()

            @pl.when((c == j % ns) & ((z != i) | (x != j // ns)))
            def _():
                out_copy(s, 0, i, j).wait_send()


def on_device(engagement, pattern, degree):
    n, nb, ns = lax.axis_size("user"), lax.axis_size("blk"), lax.axis_size("sub")
    rows, width = engagement.shape
    tiles = pattern.shape[0]
    assert n == nb * ns and ns == 2
    chunks = 4
    npairs = n * (n - 1) // 2
    block = (width, width)
    scratch = [
        pltpu.VMEM((rows, width), jnp.bfloat16),
        pltpu.VMEM((n, rows, width), jnp.bfloat16),
        pltpu.VMEM((npairs,) + block, jnp.float32),
        pltpu.VMEM((npairs,) + block, jnp.float32),
        pltpu.VMEM(block, jnp.float32),
        pltpu.VMEM((2 * nb,) + block, jnp.float32),
        pltpu.SemaphoreType.DMA((2,)),
        pltpu.SemaphoreType.DMA((2, chunks)),
        pltpu.SemaphoreType.DMA((n, chunks)),
        pltpu.SemaphoreType.DMA((npairs,)),
        pltpu.SemaphoreType.DMA((npairs,)),
        pltpu.SemaphoreType.DMA((npairs,)),
        pltpu.SemaphoreType.DMA((2 * nb,)),
        pltpu.SemaphoreType.DMA,
    ]
    vmem = pl.BlockSpec(memory_space=pltpu.VMEM)
    return pl.pallas_call(
        functools.partial(kernel, n, nb, ns, chunks),
        out_shape=jax.ShapeDtypeStruct(block, jnp.float32),
        in_specs=[pl.BlockSpec(memory_space=pl.ANY), vmem, vmem],
        out_specs=vmem,
        scratch_shapes=scratch,
        compiler_params=pltpu.CompilerParams(
            collective_id=0, has_side_effects=True, vmem_limit_bytes=60 << 20
        ),
    )(engagement, pattern.T, degree.reshape(tiles, rows // tiles))


def solution(mesh):
    placed = (
        P(("grp", "blk", "sub"), "user"),
        P(("grp", "blk", "sub"), None),
        P(("grp", "blk", "sub")),
    )
    return jax.shard_map(
        on_device,
        mesh=mesh,
        in_specs=placed,
        out_specs=P(("grp", "user"), ("blk", "sub")),
        check_vma=False,
    )
```

```python
import functools

import jax
import jax.numpy as jnp
from jax import lax
from jax.experimental import pallas as pl
from jax.experimental.pallas import tpu as pltpu
from jax.sharding import PartitionSpec as P

MESH = pl.DeviceIdType.MESH


def contract(first, second):
    return lax.dot_general(
        first, second, (((0,), (0,)), ((), ())), preferred_element_type=jnp.float32
    )


def pair_slot(n, i, j):
    return i * n - (i * (i + 1)) // 2 + (j - i - 1)


def kernel(
    n, nb, ns, chunks, eng_hbm, pattern_ref, degree_ref, out_ref,
    eng, left, acc, other, diag, landed,
    load_sem, in_send, in_recv, core_send, core_recv, out_send, out_recv, diag_send,
):
    g, z = lax.axis_index("grp"), lax.axis_index("user")
    x, c = lax.axis_index("blk"), lax.axis_index("sub")
    rows, width = eng.shape
    tiles = degree_ref.shape[0]
    tile = rows // tiles
    half = rows // 2
    step = half // chunks
    procs = (n // 2 - 1, n // 2)
    column = x * ns + c
    is_proc = (z == procs[0]) | (z == procs[1])

    first = jnp.where((z < procs[0]) | (z == procs[1]), 0, 1)

    def load(p, k):
        at = pl.ds(pl.multiple_of(p * half + k * step, step), step)
        return pltpu.make_async_copy(eng_hbm.at[at, :], eng.at[at, :], load_sem.at[p, k])

    for p in (first, 1 - first):
        for k in range(chunks):
            load(p, k).start()

    barrier = pltpu.get_barrier_semaphore()

    def sends(source, target):
        (sz, sx, sc), (tz, tx, tc) = source, target
        source_proc = (sz == procs[0]) | (sz == procs[1])
        target_proc = (tz == procs[0]) | (tz == procs[1])
        block = target_proc & (sx == tx) & (sc == tc)
        core = source_proc & (sz == tz) & (sx == tx)
        pair = source_proc & (sc == tc) & (tz < tx * ns + tc)
        own = (sz == tz) & (tz == tx * ns + tc)
        same = (sz == tz) & (sx == tx) & (sc == tc)
        return (block | core | pair | own) & jnp.logical_not(same)

    def greet(k, count):
        device = (k // (nb * ns), (k // ns) % nb, k % ns)

        @pl.when(sends(device, (z, x, c)))
        def _():
            pl.semaphore_signal(barrier, inc=1, device_id=(g,) + device, device_id_type=MESH)

        return count + jnp.where(sends((z, x, c), device), 1, 0)

    targets = lax.fori_loop(0, n * nb * ns, greet, 0)

    mask = pattern_ref[pl.ds(z, 1), :].astype(jnp.float32)
    weight = jnp.sqrt(lax.rsqrt(degree_ref[...].astype(jnp.float32)))
    weight = (weight * float(rows * nb * ns) ** (-0.25)).T * mask

    def prepare(p, k):
        start = p * half + k * step
        for t in range(start // tile, (start + step) // tile):
            at = pl.ds(t * tile, tile)
            scaled = eng[at, :].astype(jnp.float32) * weight[:, t : t + 1]
            left[z, at, :] = scaled.astype(jnp.bfloat16)

    def block_copy(source, p, k):
        at = pl.ds(p * half + k * step, step)
        return pltpu.make_async_remote_copy(
            src_ref=left.at[source, at, :],
            dst_ref=left.at[source, at, :],
            send_sem=in_send.at[p, k],
            recv_sem=in_recv.at[source, k],
            device_id=(g, procs[p], x, c),
            device_id_type=MESH,
        )

    def send_half(p, k, greeted):
        load(p, k).wait()
        prepare(p, k)
        if not greeted:
            pl.semaphore_wait(barrier, targets)

        @pl.when(z != procs[p])
        def _():
            block_copy(z, p, k).start()

    for p in range(2):

        @pl.when(first == p)
        def _():
            for k in range(chunks):
                send_half(p, k, k > 0)
            for k in range(chunks):
                send_half(1 - p, k, True)

    def diag_copy(slot):
        return pltpu.make_async_remote_copy(
            src_ref=diag,
            dst_ref=landed.at[slot],
            send_sem=diag_send,
            recv_sem=out_recv.at[slot],
            device_id=(g, z, z // ns, lax.rem(z, ns)),
            device_id_type=MESH,
        )

    diag[...] = contract(left[z], left[z])

    @pl.when(column != z)
    def _():
        diag_copy(c * nb + x).start()

    def core_copy(s):
        return pltpu.make_async_remote_copy(
            src_ref=acc.at[s],
            dst_ref=other.at[s],
            send_sem=core_send.at[s],
            recv_sem=core_recv.at[s],
            device_id=(g, z, x, 1 - c),
            device_id_type=MESH,
        )

    def out_copy(s, slot, i, j):
        return pltpu.make_async_remote_copy(
            src_ref=acc.at[s],
            dst_ref=landed.at[slot],
            send_sem=out_send.at[s],
            recv_sem=out_recv.at[slot],
            device_id=(g, i, j // ns, c),
            device_id_type=MESH,
        )

    def pairs_of(p, blocks, pairs):
        for i, j in pairs:
            s = pair_slot(n, i, j)
            acc[s] = jnp.zeros_like(acc[s])

        def multiply(k, carry):
            for i in blocks:
                block_copy(i, p, k).wait_recv()
            at = pl.ds(pl.multiple_of(p * half + k * step, 16), step)
            for i, j in pairs:
                acc[pair_slot(n, i, j)] += contract(left[i, at, :], left[j, at, :])
            return carry

        lax.fori_loop(0, chunks, multiply, 0)

        for i, j in pairs:

            @pl.when(c != j % ns)
            def _():
                core_copy(pair_slot(n, i, j)).start()

        for i, j in pairs:
            s = pair_slot(n, i, j)

            @pl.when(c == j % ns)
            def _():
                core_copy(s).wait_recv()
                acc[s] += other[s]

                @pl.when((procs[p] != i) | (x != j // ns))
                def _():
                    out_copy(s, p * nb + x, i, j).start()

    pairs = [(i, j) for i in range(n) for j in range(i + 1, n)]
    for p in range(2):

        @pl.when(z == procs[p])
        def _():
            below, above = range(procs[0]), range(procs[1] + 1, n)
            near, far = (below, above) if p == 0 else (above, below)
            early = [pair for pair in pairs if not set(pair) & set(far)]
            late = sorted((pair for pair in pairs if set(pair) & set(far)), key=lambda pair: abs(pair[0] - procs[p]), reverse=True)
            pairs_of(p, [*near, procs[1 - p]], early)
            if late:
                pairs_of(p, far, late)

    @pl.when(column < z)
    def _():
        out_ref[...] = jnp.zeros_like(out_ref)

    @pl.when(column == z)
    def _():
        out_ref[...] = diag[...]
        for cc in range(ns):
            for xx in range(nb):

                @pl.when((xx != x) | (cc != c))
                def _():
                    slot = cc * nb + xx
                    diag_copy(slot).wait_recv()
                    out_ref[...] += landed[slot]

    @pl.when(column > z)
    def _():
        out_ref[...] = jnp.zeros_like(out_ref)

        @pl.when(is_proc)
        def _():
            out_ref[...] = acc[pair_slot(n, z, column)]

        for p in range(2):
            for xx in range(nb):

                @pl.when((z != procs[p]) | (xx != x))
                def _():
                    slot = p * nb + xx
                    out_copy(0, slot, z, column).wait_recv()
                    out_ref[...] += landed[slot]

    for k in range(chunks):
        for p in range(2):

            @pl.when(z != procs[p])
            def _():
                block_copy(z, p, k).wait_send()

    @pl.when(column != z)
    def _():
        diag_copy(0).wait_send()

    @pl.when(is_proc)
    def _():
        for s, (i, j) in enumerate(pairs):

            @pl.when(c != j % ns)
            def _():
                core_copy(s).wait_send()

            @pl.when((c == j % ns) & ((z != i) | (x != j // ns)))
            def _():
                out_copy(s, 0, i, j).wait_send()


def on_device(engagement, pattern, degree):
    n, nb, ns = lax.axis_size("user"), lax.axis_size("blk"), lax.axis_size("sub")
    rows, width = engagement.shape
    tiles = pattern.shape[0]
    assert n == nb * ns and ns == 2
    chunks = 3
    npairs = n * (n - 1) // 2
    block = (width, width)
    scratch = [
        pltpu.VMEM((rows, width), jnp.bfloat16),
        pltpu.VMEM((n, rows, width), jnp.bfloat16),
        pltpu.VMEM((npairs,) + block, jnp.float32),
        pltpu.VMEM((npairs,) + block, jnp.float32),
        pltpu.VMEM(block, jnp.float32),
        pltpu.VMEM((2 * nb,) + block, jnp.float32),
        pltpu.SemaphoreType.DMA((2, chunks)),
        pltpu.SemaphoreType.DMA((2, chunks)),
        pltpu.SemaphoreType.DMA((n, chunks)),
        pltpu.SemaphoreType.DMA((npairs,)),
        pltpu.SemaphoreType.DMA((npairs,)),
        pltpu.SemaphoreType.DMA((npairs,)),
        pltpu.SemaphoreType.DMA((2 * nb,)),
        pltpu.SemaphoreType.DMA,
    ]
    vmem = pl.BlockSpec(memory_space=pltpu.VMEM)
    result = pl.pallas_call(
        functools.partial(kernel, n, nb, ns, chunks),
        out_shape=jax.ShapeDtypeStruct(block, jnp.float32),
        in_specs=[pl.BlockSpec(memory_space=pl.ANY), vmem, vmem],
        out_specs=vmem,
        scratch_shapes=scratch,
        compiler_params=pltpu.CompilerParams(
            collective_id=0, has_side_effects=True, vmem_limit_bytes=58 << 20
        ),
    )(engagement, pattern.T, degree.reshape(tiles, rows // tiles))
    column = lax.axis_index("blk") * ns + lax.axis_index("sub")
    return jnp.where(column >= lax.axis_index("user"), result, jnp.float32(0.0))


def solution(mesh):
    placed = (
        P(("grp", "blk", "sub"), "user"),
        P(("grp", "blk", "sub"), None),
        P(("grp", "blk", "sub")),
    )
    return jax.shard_map(
        on_device,
        mesh=mesh,
        in_specs=placed,
        out_specs=P(("grp", "user"), ("blk", "sub")),
        check_vma=False,
    )
```
